32 devices in a mesh: line: 8 (over y, x, core), batch: 4 (over z).
Axes of the slice: x: 2, y: 2, z: 4, core: 2. Of those that a mesh axis runs over, the one named last changes fastest.
Arguments:
- conserved: float32 [6, 192, 8, 1024], P(None, 'line', None, 'batch'), may hold values from -6 to 6
- flux_matrix: float32 [6, 6], replicated, may hold values from -2.5 to 2.5
- speed_xi: float32 [192, 8, 1024], P('line', None, 'batch'), may hold values from 0.2 to 2
- speed_eta: float32 [192, 8, 1024], P('line', None, 'batch'), may hold values from 0.2 to 2
- x_low1: float32 [192, 8, 1024], P('line', None, 'batch'), may hold values from -111 to -54
- x_low2: float32 [192, 8, 1024], P('line', None, 'batch'), may hold values from -1 to 1
- x_dinv: float32 [192, 8, 1024], P('line', None, 'batch'), may hold values from 0.009 to 0.018
- x_up1: float32 [192, 8, 1024], P('line', None, 'batch'), may hold values from -0.99 to -0.965
- x_up2: float32 [192, 8, 1024], P('line', None, 'batch'), may hold values from -0.008 to 0.008
- e_low1: float32 [192, 8, 1024], P('line', None, 'batch'), may hold values from -0.6 to -0.3
- e_low2: float32 [192, 8, 1024], P('line', None, 'batch'), may hold values from -0.2 to 0.2
- e_dinv: float32 [192, 8, 1024], P('line', None, 'batch'), may hold values from 0.6 to 0.9
- e_up1: float32 [192, 8, 1024], P('line', None, 'batch'), may hold values from -0.6 to -0.3
- e_up2: float32 [192, 8, 1024], P('line', None, 'batch'), may hold values from -0.2 to 0.2
- donor_index: int32 [8, 65536], P(None, ('line', 'batch')), may hold values from 0 to 32703
- donor_weight: float32 [8, 65536], P(None, ('line', 'batch')), may hold values from 0.05 to 0.25
- receive_index: int32 [65536], P(('line', 'batch')), may hold values from 0 to 49152, as said below
Outputs:
- updated: float32 [6, 192, 8, 1024], P(None, 'line', None, 'batch')
The draws below stay inside these ranges and needn't reach their ends.
Inputs may be any that keep to these rules, and one draw needn't show every extreme that they name: `receive_index`: live cells of one device are distinct; the live slots of each pair of devices come first and the others hold 49152; some device receives all 64 slots from every device.
All inputs are finite; a program needn't handle non-finite values.
Results may differ from the reference program's by a relative error of at most 0.0001.
Values sent between devices are 32-bit elements; how exact they have to be, the bound alone decides.
No kernel may reach another device: no remote copies, remote signals or barrier semaphores. Data moves between devices by JAX's collectives and lax.ppermute only.
A program may use at most 192 MiB of HBM per device.

```python
import math
import jax
import jax.numpy as jnp
from jax import lax

FIELDS = 6
CL = 24
NE = 8
LB = 256
SLOT = 64
SUBITERS = 2
CELLS = 49152
FRINGE = 2048
NL = 192
NB = 1024
N_LINE = 8
N_BATCH = 4
DEVICES = 32


def draw_receive_index(key, part):
    key = jax.random.fold_in(key, 7)
    devices = FRINGE // SLOT
    keys = jax.random.split(jax.random.fold_in(key, 1), devices)
    cells = jax.vmap(lambda k: jax.random.permutation(k, CELLS)[:FRINGE])(keys)
    counts = jax.random.randint(jax.random.fold_in(key, 2), (devices, devices), 1, SLOT + 1)
    fullest = jax.random.randint(jax.random.fold_in(key, 3), (), 0, devices)
    counts = jnp.where(jnp.arange(devices)[:, None] == fullest, SLOT, counts)
    live = jnp.arange(SLOT)[None, None, :] < counts[:, :, None]
    result = jnp.where(live.reshape(devices, FRINGE), cells, CELLS)
    return result.reshape(-1).astype(jnp.int32)


def line_factors(key, low_inv, high_inv, low_rate, high_rate, coupling):
    shape = (NL, NE, NB)
    inv_key = jax.random.fold_in(key, 31)
    rate_key = jax.random.fold_in(key, 32)
    couple_key = jax.random.fold_in(key, 33)
    spread = jax.random.uniform(inv_key, shape, jnp.float32)
    inverse = low_inv * jnp.exp(spread * jnp.log(jnp.float32(high_inv / low_inv)))
    rate = jax.random.uniform(rate_key, shape, jnp.float32, low_rate, high_rate)
    couple = jax.random.uniform(couple_key, shape, jnp.float32, -coupling, coupling)
    return (inverse, rate, couple)


def draw_x_dinv(key, part):
    inverse, rate, couple = line_factors(key, 0.012, 0.018, 0.975, 0.985, 0.012)
    return inverse.astype(jnp.float32)


def draw_x_low1(key, part):
    inverse, rate, couple = line_factors(key, 0.012, 0.018, 0.975, 0.985, 0.012)
    return (-rate / inverse).astype(jnp.float32)


def draw_x_low2(key, part):
    inverse, rate, couple = line_factors(key, 0.012, 0.018, 0.975, 0.985, 0.012)
    return (couple / inverse).astype(jnp.float32)


def touch_ends(entries, key, low, high):
    longest = entries.shape.index(max(entries.shape))
    spots = []
    for shift in (0, 1):
        where = [jax.random.randint(jax.random.fold_in(key, axis), (), 0, length) for axis, length in enumerate(entries.shape)]
        where[longest] = (where[longest] + shift) % entries.shape[longest]
        spots.append(tuple(where))
    return entries.at[spots[0]].set(low).at[spots[1]].set(high)


def steps_of(rng, extent, cuts, least, largest):
    level, own = 1.0, jax.random.fold_in(rng, 6)
    for position, shards_of in cuts:
        steps = jnp.exp(jax.random.uniform(jax.random.fold_in(own, position), (shards_of,), jnp.float32, least / len(cuts), largest / len(cuts)))
        level = level * jnp.repeat(steps, extent[position] // shards_of).reshape([-1 if axis == position else 1 for axis in range(len(extent))])
    return level


def noise(key, dims, deviation, limit, pieces=(), dtype=jnp.bfloat16):
    level = steps_of(key, dims, pieces, -0.22, 0.18) if pieces else 1.0
    values = jax.random.normal(key, dims, jnp.float32) * deviation * level
    return jnp.minimum(jnp.maximum(values, -limit), limit).astype(dtype)


def setup_inputs(seed: int = 0) -> dict:
    arg_keys = jax.random.split(jax.random.key(seed), 18)
    return {
        "conserved": noise(arg_keys[0], (FIELDS, NL, NE, NB), 1.0, 6.0, ((1, 8), (3, 4)), jnp.float32),
        "flux_matrix": noise(arg_keys[1], (FIELDS, FIELDS), FIELDS ** -0.5, 2.5, (), jnp.float32),
        "speed_xi": jnp.clip(jnp.exp(math.log(2.0) - 2.3025851 * jax.random.uniform(arg_keys[2], (NL, NE, NB), jnp.float32) ** steps_of(arg_keys[2], (NL, NE, NB), ((0, 8), (2, 4)), -0.2, 0.2)), 0.2, 2.0),
        "speed_eta": jnp.clip(jnp.exp(math.log(2.0) - 2.3025851 * jax.random.uniform(arg_keys[3], (NL, NE, NB), jnp.float32) ** steps_of(arg_keys[3], (NL, NE, NB), ((0, 8), (2, 4)), -0.2, 0.2)), 0.2, 2.0),
        "x_low1": draw_x_low1(jax.random.fold_in(arg_keys[17], 71), 0),
        "x_low2": draw_x_low2(jax.random.fold_in(arg_keys[17], 71), 0),
        "x_dinv": draw_x_dinv(jax.random.fold_in(arg_keys[17], 71), 0),
        "x_up1": jnp.clip(-0.99 + 0.025000036 * jax.random.uniform(arg_keys[7], (NL, NE, NB), jnp.float32) ** steps_of(arg_keys[7], (NL, NE, NB), ((0, 8), (2, 4)), -0.2, 0.2), -0.99, -0.965),
        "x_up2": jnp.clip(jax.random.uniform(arg_keys[8], (NL, NE, NB), jnp.float32, -0.008, 0.008) * steps_of(arg_keys[8], (NL, NE, NB), ((0, 8), (2, 4)), -0.4, 0.0), -0.008, 0.008),
        "e_low1": jnp.clip(-0.6 + 0.3 * jax.random.uniform(arg_keys[9], (NL, NE, NB), jnp.float32) ** steps_of(arg_keys[9], (NL, NE, NB), ((0, 8), (2, 4)), -0.2, 0.2), -0.6, -0.3),
        "e_low2": jnp.clip(jax.random.uniform(arg_keys[10], (NL, NE, NB), jnp.float32, -0.2, 0.2) * steps_of(arg_keys[10], (NL, NE, NB), ((0, 8), (2, 4)), -0.4, 0.0), -0.2, 0.2),
        "e_dinv": jnp.clip(jnp.exp(math.log(0.9) - 0.40546504 * jax.random.uniform(arg_keys[11], (NL, NE, NB), jnp.float32) ** steps_of(arg_keys[11], (NL, NE, NB), ((0, 8), (2, 4)), -0.2, 0.2)), 0.6, 0.9),
        "e_up1": jnp.clip(-0.6 + 0.3 * jax.random.uniform(arg_keys[12], (NL, NE, NB), jnp.float32) ** steps_of(arg_keys[12], (NL, NE, NB), ((0, 8), (2, 4)), -0.2, 0.2), -0.6, -0.3),
        "e_up2": jnp.clip(jax.random.uniform(arg_keys[13], (NL, NE, NB), jnp.float32, -0.2, 0.2) * steps_of(arg_keys[13], (NL, NE, NB), ((0, 8), (2, 4)), -0.4, 0.0), -0.2, 0.2),
        "donor_index": touch_ends(jax.random.randint(arg_keys[14], (8, DEVICES * FRINGE), 0, min(CELLS, 32704)), jax.random.fold_in(arg_keys[14], 1), 0, (min(CELLS, 32704)) - 1).astype(jnp.int32),
        "donor_weight": jnp.clip(0.05 + 0.2 * jax.random.uniform(arg_keys[15], (8, DEVICES * FRINGE), jnp.float32) ** steps_of(arg_keys[15], (8, DEVICES * FRINGE), ((1, 32),), -0.2, 0.2), 0.05, 0.25),
        "receive_index": draw_receive_index(jax.random.fold_in(arg_keys[17], 71), 0),
    }


dissip = 0.02
step_size = 0.1


def residual(field, start, flux_matrix, speed_xi, speed_eta):
    flux = jnp.einsum("cd,dijk->cijk", flux_matrix, field, precision=lax.Precision.HIGHEST)
    flux_pad = jnp.pad(flux, ((0, 0), (1, 1), (1, 1), (0, 0)))
    d_xi = 0.5 * (flux_pad[:, 2:, 1:-1] - flux_pad[:, :-2, 1:-1])
    d_eta = 0.5 * (flux_pad[:, 1:-1, 2:] - flux_pad[:, 1:-1, :-2])
    padded = jnp.pad(field, ((0, 0), (2, 2), (2, 2), (0, 0)))
    centre = padded[:, 2:-2, 2:-2]
    fourth_xi = padded[:, :-4, 2:-2] - 4.0 * padded[:, 1:-3, 2:-2] + 6.0 * centre - 4.0 * padded[:, 3:-1, 2:-2] + padded[:, 4:, 2:-2]
    fourth_eta = padded[:, 2:-2, :-4] - 4.0 * padded[:, 2:-2, 1:-3] + 6.0 * centre - 4.0 * padded[:, 2:-2, 3:-1] + padded[:, 2:-2, 4:]
    return -(speed_xi * d_xi + speed_eta * d_eta) - dissip * (fourth_xi + fourth_eta) - (field - start)


def lower_sweep(right, first, second, inverse):
    zero = jnp.zeros(right.shape[1:], jnp.float32)

    def advance(carry, items):
        prev_one, prev_two = carry
        value, coef_one, coef_two, coef_inv = items
        new = coef_inv * (value - coef_one * prev_one - coef_two * prev_two)
        return (new, prev_one), new

    _, result = lax.scan(advance, (zero, zero), (right, first, second, inverse))
    return result


def upper_sweep(right, first, second):
    zero = jnp.zeros(right.shape[1:], jnp.float32)

    def advance(carry, items):
        next_one, next_two = carry
        value, coef_one, coef_two = items
        new = value - coef_one * next_one - coef_two * next_two
        return (new, next_one), new

    _, result = lax.scan(advance, (zero, zero), (right, first, second), reverse=True)
    return result


def fringe(field, donor_index, donor_weight, receive_index):
    devices = N_LINE * N_BATCH
    blocks = field.reshape(FIELDS, N_LINE, CL, NE, N_BATCH, LB).transpose(1, 4, 0, 2, 3, 5).reshape(devices, FIELDS, CELLS)
    index = donor_index.reshape(8, devices, FRINGE).transpose(1, 0, 2)
    weight = donor_weight.reshape(8, devices, FRINGE).transpose(1, 0, 2)

    def interpolate(items):
        block, cells, weights = items
        picked = block[:, cells]
        return jnp.sum(picked * weights[None], axis=1)

    values = lax.map(interpolate, (blocks, index, weight))
    inbound = values.reshape(devices, FIELDS, devices, SLOT).transpose(2, 1, 0, 3).reshape(devices, FIELDS, FRINGE)
    targets = receive_index.reshape(devices, FRINGE)

    def place(block, cells, incoming):
        return block.at[:, cells].set(incoming, mode="drop")

    blocks = jax.vmap(place)(blocks, targets, inbound)
    return blocks.reshape(N_LINE, N_BATCH, FIELDS, CL, NE, LB).transpose(2, 0, 3, 4, 1, 5).reshape(FIELDS, NL, NE, NB)


def reference(conserved, flux_matrix, speed_xi, speed_eta, x_low1, x_low2, x_dinv, x_up1, x_up2, e_low1, e_low2, e_dinv, e_up1, e_up2, donor_index, donor_weight, receive_index):
    field = conserved
    eta_coefs = [jnp.moveaxis(c, 1, 0) for c in (e_low1, e_low2, e_dinv, e_up1, e_up2)]
    for sweep in range(SUBITERS):
        field = fringe(field, donor_index, donor_weight, receive_index)
        rhs = step_size * residual(field, conserved, flux_matrix, speed_xi, speed_eta)
        lines = jnp.moveaxis(rhs, 1, 0)
        lines = upper_sweep(lower_sweep(lines, x_low1, x_low2, x_dinv), x_up1, x_up2)
        across = jnp.moveaxis(jnp.moveaxis(lines, 0, 1), 2, 0)
        across = upper_sweep(lower_sweep(across, eta_coefs[0], eta_coefs[1], eta_coefs[2]), eta_coefs[3], eta_coefs[4])
        field = field + jnp.moveaxis(across, 0, 2)
    return field
```

```python
import functools

import jax
import jax.numpy as jnp
from jax import lax
from jax.experimental import pallas as pl
from jax.experimental.pallas import tpu as pltpu
from jax.sharding import PartitionSpec as P

SUBITERS = 2
DISSIP = 0.02
STEP = 0.1

SUB = 8
LANES = 128
HALO = 2
SLOTS = 4

VM = pl.BlockSpec(memory_space=pltpu.VMEM)
SM = pl.BlockSpec(memory_space=pltpu.SMEM)
F32 = jnp.float32
I32 = jnp.int32


def f32(*shape):
    return jax.ShapeDtypeStruct(shape, F32)


class Sizes:
    def __init__(self, fields, cl, ne, lb):
        assert fields <= SUB and ne == SUB and lb % LANES == 0
        self.fields, self.cl, self.ne, self.lb = fields, cl, ne, lb
        self.halves = lb // LANES
        self.columns = self.halves * ne
        self.layer = self.columns * SUB
        self.rows = (cl + 2 * HALO) * self.layer
        assert lb & (lb - 1) == 0

    def at(self, i, h, j):
        return ((i * self.halves + h) * SUB + j) * SUB

    def row_of_cell(self, cell):
        k_bits = self.lb.bit_length() - 1
        half = (cell & (self.lb - 1)) >> 7
        j = (cell >> k_bits) & (SUB - 1)
        i = cell >> (k_bits + 3)
        return ((i + HALO) * self.halves + half) * (SUB * SUB) + j * SUB


def grid_of(axis):
    return lax.broadcasted_iota(I32, (SUB, LANES), axis)


def swap_corners(block):
    keep = (grid_of(0) < 4) == (grid_of(1) < LANES // 2)
    return jnp.where(keep, block, pltpu.roll(pltpu.roll(block, 4, 0), LANES // 2, 1))


def total(parts):
    parts = list(parts)
    while len(parts) > 1:
        parts = [parts[i] + parts[i + 1] if i + 1 < len(parts) else parts[i] for i in range(0, len(parts), 2)]
    return parts[0]


def gather_block(slots, block, donor, weight, tiles, out, picks):
    corners = donor.shape[0]
    lane = grid_of(1)
    down = lax.broadcasted_iota(I32, (LANES, LANES), 0)
    base = pl.multiple_of(block * LANES, LANES)
    for k in range(corners):
        cell = donor[k : k + 1, pl.ds(base, LANES)] & (LANES - 1)
        chosen = jnp.where(down == cell, weight[k : k + 1, pl.ds(base, LANES)], 0.0)
        picks[k * LANES : (k + 1) * LANES, :] = chosen.T
    result = jnp.zeros((SUB, LANES), F32)
    for n in range(LANES):
        parts = []
        for k in range(corners):
            row = pl.multiple_of(slots[k, n], SUB)
            parts.append(tiles[pl.ds(row, SUB), :] * picks[k * LANES + n : k * LANES + n + 1, :])
        result = jnp.where(lane == n, jnp.sum(total(parts), axis=1, keepdims=True), result)
    out[pl.ds(pl.multiple_of(block * SUB, SUB), SUB), :] = swap_corners(result)


def gather_all(z, donor, weight, tiles, out, picks, where, slots, sems):
    blocks = donor.shape[1] // LANES
    where[...] = z.row_of_cell(donor[...])

    def fetch(block, slot):
        source = where.at[:, pl.ds(pl.multiple_of(block * LANES, LANES), LANES)]
        return pltpu.make_async_copy(source, slots[slot], sems.at[slot])

    for slot in range(SLOTS):
        fetch(slot, slot).start()

    def lap(turn, carry):
        for slot in range(SLOTS):
            block = SLOTS * turn + slot
            fetch(block, slot).wait()
            gather_block(slots[slot], block, donor, weight, tiles, out, picks)

            @pl.when(block + SLOTS < blocks)
            def _():
                fetch(block + SLOTS, slot).start()

        return carry

    lax.fori_loop(0, blocks // SLOTS, lap, 0)


def gather_scratch(corners, count):
    return [
        pltpu.VMEM((corners * LANES, LANES), F32),
        pltpu.VMEM((corners, count), I32),
        *[pltpu.SMEM((corners, LANES), I32) for _ in range(SLOTS)],
        pltpu.SemaphoreType.DMA((SLOTS,)),
    ]


def first_kernel(z, donor, weight, conserved, out, tiles_out, tiles, picks, where, *rest):
    slots, sems = rest[:SLOTS], rest[SLOTS]
    tiles[...] = jnp.zeros(tiles.shape, F32)
    for f in range(z.fields):
        for i in range(z.cl):
            for h in range(z.halves):
                block = conserved[f, i, :, h * LANES : (h + 1) * LANES]
                tiles[pl.ds(z.at(i + HALO, h, 0) + f, SUB, stride=SUB), :] = block
    gather_all(z, donor, weight, tiles, out, picks, where, slots, sems)
    tiles_out[...] = tiles[...]


def place_kernel(z, place, receive, inbound, tiles, out, same_chip, next_chip, row_v, lane_v, row_s, lane_s, sems):
    blocks = receive.shape[0]
    lane = grid_of(1)
    cell = receive[...]
    row_v[...] = z.row_of_cell(cell)
    lane_v[...] = cell & (LANES - 1)
    rows = pltpu.make_async_copy(row_v, row_s, sems.at[0])
    lanes = pltpu.make_async_copy(lane_v, lane_s, sems.at[1])
    rows.start()
    lanes.start()
    out[...] = tiles[...]
    rows.wait()
    lanes.wait()

    def lap(block, carry):
        values = swap_corners(inbound[pl.ds(pl.multiple_of(block * SUB, SUB), SUB), :])
        for n in range(LANES):
            row = pl.multiple_of(row_s[block, n], SUB)
            column = jnp.broadcast_to(values[:, n : n + 1], (SUB, LANES))
            pltpu.store(out.at[pl.ds(row, SUB), :], column, mask=lane == lane_s[block, n])
        return carry

    lax.fori_loop(0, blocks, lap, 0)
    core = place[1]
    low, high = HALO * z.layer, z.cl * z.layer
    same_chip[...] = out[pl.ds(pl.multiple_of(jnp.where(core == 0, high, low), SUB), HALO * z.layer), :]
    next_chip[...] = out[pl.ds(pl.multiple_of(jnp.where(core == 0, low, high), SUB), HALO * z.layer), :]


def line_of(ref, i, h, j):
    return ref[i, j : j + 1, h * LANES : (h + 1) * LANES]


def lower_at(z, rhs, low1, low2, dinv, keep, state, i, h, j):
    row = z.at(i, h, j)
    one, two = state
    new = line_of(dinv, i, h, j) * (
        rhs[row : row + SUB, :] - line_of(low1, i, h, j) * one - line_of(low2, i, h, j) * two
    )
    keep[row : row + SUB, :] = new
    return (new, one)


def upper_at(z, keep, up1, up2, state, i, h, j):
    row = z.at(i, h, j)
    one, two = state
    new = keep[row : row + SUB, :] - line_of(up1, i, h, j) * one - line_of(up2, i, h, j) * two
    return (new, one)


def segment_kernel(z, low1, low2, dinv, up1, up2, out):
    for h in range(z.halves):
        cut = slice(h * LANES, (h + 1) * LANES)
        zero, one = jnp.zeros((SUB, LANES), F32), jnp.ones((SUB, LANES), F32)
        planes = [None] * 12
        for unit in range(2):
            a, b = (one, zero) if unit == 0 else (zero, one)
            kept = []
            for i in range(z.cl):
                a, b = -dinv[i, :, cut] * (low1[i, :, cut] * a + low2[i, :, cut] * b), a
                kept.append(a)
            planes[unit], planes[2 + unit] = a, b
            a, b = zero, zero
            for i in reversed(range(z.cl)):
                a, b = kept[i] - up1[i, :, cut] * a - up2[i, :, cut] * b, a
            planes[4 + unit], planes[6 + unit] = a, b
            a, b = (one, zero) if unit == 0 else (zero, one)
            for i in reversed(range(z.cl)):
                a, b = -up1[i, :, cut] * a - up2[i, :, cut] * b, a
            planes[8 + unit], planes[10 + unit] = a, b
        for p in range(12):
            row = p * z.columns + h * SUB
            out[row : row + SUB, :] = planes[p]


def residual_kernel(
    z, place, tiles, start, same_chip, next_chip, speed_xi, speed_eta, matrix,
    low1, low2, dinv, up1, up2, rhs, ends, field, slope, keep, spread,
):
    first = place[1] == 0
    edge = HALO * z.layer
    field[edge : edge + z.cl * z.layer, :] = tiles[edge : edge + z.cl * z.layer, :]
    field[0:edge, :] = jnp.where(first, next_chip[...], same_chip[...])
    field[z.rows - edge : z.rows, :] = jnp.where(first, same_chip[...], next_chip[...])
    columns = [jnp.broadcast_to(matrix[:, d : d + 1] * (-0.5 * STEP), (SUB, LANES)) for d in range(z.fields)]
    nothing = jnp.zeros((SUB, LANES), F32)

    def layer(i, carry):
        base = pl.multiple_of((i + HALO) * z.layer, SUB)

        def point(step, h, j):
            if j < 0 or j >= SUB:
                return nothing
            return field[pl.ds(base + step * z.layer + z.at(0, h, j), SUB), :]

        for h in range(z.halves):
            for j in range(SUB):
                row = z.at(0, h, j)
                centre = point(0, h, j)
                before, after = point(-1, h, j), point(1, h, j)
                under, over = point(0, h, j - 1), point(0, h, j + 1)
                change = line_of(speed_xi, i, h, j) * (after - before) + line_of(speed_eta, i, h, j) * (over - under)
                slope[row : row + SUB, :] = change
                near = (before + after) + (under + over)
                far = (point(-2, h, j) + point(2, h, j)) + (point(0, h, j - 2) + point(0, h, j + 2))
                fourth = far - 4.0 * near + 12.0 * centre
                value = -(STEP * DISSIP) * fourth - STEP * (centre - start[pl.ds(base + row, SUB), :])
                value = value + total(
                    [columns[d] * slope[row + d : row + d + 1, :] for d in range(z.fields)]
                )
                rhs[pl.ds(pl.multiple_of(i * z.layer, SUB) + row, SUB), :] = value
        return carry

    lax.fori_loop(0, z.cl, layer, 0)
    for h in range(z.halves):
        states = [(nothing, nothing)] * SUB
        for i in range(z.cl):
            states = [lower_at(z, rhs, low1, low2, dinv, keep, states[j], i, h, j) for j in range(SUB)]
        lowered = states
        states = [(nothing, nothing)] * SUB
        for i in reversed(range(z.cl)):
            states = [upper_at(z, keep, up1, up2, states[j], i, h, j) for j in range(SUB)]
        for j in range(SUB):
            for v, value in enumerate((*lowered[j], *states[j])):
                spread[pl.ds(v * z.columns + h * SUB + j, SUB, stride=4 * z.columns), :] = value
    ends[...] = spread[0 : z.fields * 4 * z.columns, :]


def solve_kernel(z, count, last, *refs):
    pairs = count // 2
    place, refs = refs[0], refs[1:]
    ends, maps, refs = refs[:count], refs[count : 2 * count], refs[2 * count :]
    (rhs, tiles, low1, low2, dinv, up1, up2, e_low1, e_low2, e_dinv, e_up1, e_up2), refs = refs[:12], refs[12:]
    if last:
        out, states, planes, spread, keep, fresh = refs
    else:
        donor, weight, out, tiles_out, states, planes, spread, keep, fresh, picks, where, *rest = refs
    me, core, chip = place[0], place[1], place[2]
    s_rows, m_rows = ends[0].shape[0], maps[0].shape[0]
    for s in range(pairs):
        for other in range(2):
            device = (chip ^ s) * 2 + (core ^ other)
            states[pl.ds(pl.multiple_of(device * s_rows, SUB), s_rows), :] = ends[2 * s + other][...]
            planes[pl.ds(pl.multiple_of(device * m_rows, SUB), m_rows), :] = maps[2 * s + other][...]

    zero = jnp.zeros((SUB, LANES), F32)
    for h in range(z.halves):

        def plane(device, p):
            row = device * m_rows + p * z.columns + h * SUB
            return planes[row : row + SUB, :]

        def end(device, f, v):
            row = device * s_rows + (f * 4 + v) * z.columns + h * SUB
            return states[row : row + SUB, :]

        entering = [[(zero, zero)] for _ in range(z.fields)]
        for d in range(count - 1):
            for f in range(z.fields):
                a, b = entering[f][-1]
                entering[f].append(
                    (
                        end(d, f, 0) + plane(d, 0) * a + plane(d, 1) * b,
                        end(d, f, 1) + plane(d, 2) * a + plane(d, 3) * b,
                    )
                )
        own = [[zero] * 4 for _ in range(z.fields)]
        returning = [(zero, zero)] * z.fields
        for d in reversed(range(count)):
            for f in range(z.fields):
                a, b = entering[f][d]
                g, k = returning[f]
                own[f] = [jnp.where(me == d, new, old) for new, old in zip((a, b, g, k), own[f])]
                returning[f] = (
                    (end(d, f, 2) + plane(d, 4) * a + plane(d, 5) * b) + (plane(d, 8) * g + plane(d, 9) * k),
                    (end(d, f, 3) + plane(d, 6) * a + plane(d, 7) * b) + (plane(d, 10) * g + plane(d, 11) * k),
                )
        for f in range(SUB):
            for v in range(4):
                row = (f * 4 + v) * z.columns + h * SUB
                spread[row : row + SUB, :] = own[f][v] if f < z.fields else zero

    def enter(v, h, j):
        return spread[pl.ds(v * z.columns + h * SUB + j, SUB, stride=4 * z.columns), :]

    if not last:
        fresh[0 : HALO * z.layer, :] = jnp.zeros((HALO * z.layer, LANES), F32)
        fresh[z.rows - HALO * z.layer : z.rows, :] = jnp.zeros((HALO * z.layer, LANES), F32)
    for h in range(z.halves):
        state = [(enter(0, h, j), enter(1, h, j)) for j in range(SUB)]
        for i in range(z.cl):
            state = [lower_at(z, rhs, low1, low2, dinv, keep, state[j], i, h, j) for j in range(SUB)]
        state = [(enter(2, h, j), enter(3, h, j)) for j in range(SUB)]
        for i in reversed(range(z.cl)):
            state = [upper_at(z, keep, up1, up2, state[j], i, h, j) for j in range(SUB)]
            one, two = zero, zero
            lowered = []
            for j in range(SUB):
                new = line_of(e_dinv, i, h, j) * (
                    state[j][0] - line_of(e_low1, i, h, j) * one - line_of(e_low2, i, h, j) * two
                )
                one, two = new, one
                lowered.append(new)
            one, two = zero, zero
            for j in reversed(range(SUB)):
                new = lowered[j] - line_of(e_up1, i, h, j) * one - line_of(e_up2, i, h, j) * two
                one, two = new, one
                row = z.at(i + HALO, h, j)
                fresh[row : row + SUB, :] = tiles[row : row + SUB, :] + new
    if last:
        for f in range(z.fields):
            for i in range(z.cl):
                for h in range(z.halves):
                    out[f, i, :, h * LANES : (h + 1) * LANES] = fresh[
                        pl.ds(z.at(i + HALO, h, 0) + f, SUB, stride=SUB), :
                    ]
    else:
        gather_all(z, donor, weight, fresh, out, picks, where, rest[:SLOTS], rest[SLOTS])
        tiles_out[...] = fresh[...]


def across_line(array):
    size = lax.axis_size("line")
    chips = size // 2
    result = []
    for s in range(chips):
        there = array
        if s:
            there = lax.ppermute(array, "line", [(i, i ^ (2 * s)) for i in range(size)])
        result.append(there)
        result.append(lax.ppermute(there, "line", [(i, i ^ 1) for i in range(size)]))
    return result


def local(
    conserved, flux_matrix, speed_xi, speed_eta, x_low1, x_low2, x_dinv, x_up1, x_up2,
    e_low1, e_low2, e_dinv, e_up1, e_up2, donor_index, donor_weight, receive_index,
):
    z = Sizes(*conserved.shape)
    count = lax.axis_size("line")
    devices = count * lax.axis_size("batch")
    corners, fringe = donor_index.shape
    assert fringe == devices * (LANES // 2) and count % 2 == 0 and count & (count - 1) == 0
    blocks = fringe // LANES
    me = lax.axis_index("line").astype(I32)
    place = jnp.stack([me, me & 1, me >> 1])
    matrix = jnp.pad(flux_matrix, ((0, SUB - z.fields), (0, LANES - z.fields)))
    receive = receive_index.reshape(blocks, LANES)
    x_coefs = (x_low1, x_low2, x_dinv, x_up1, x_up2)
    e_coefs = (e_low1, e_low2, e_dinv, e_up1, e_up2)
    params = pltpu.CompilerParams(vmem_limit_bytes=32 * 1024 * 1024)
    picked = f32(blocks * SUB, LANES)
    tile_shape = f32(z.rows, LANES)
    tile_mem = pltpu.VMEM((z.rows, LANES), F32)
    inner_mem = pltpu.VMEM((z.cl * z.layer, LANES), F32)
    spread_mem = pltpu.VMEM((SUB * 4 * z.columns, LANES), F32)
    s_rows, m_rows = z.fields * 4 * z.columns, 12 * z.columns

    maps = pl.pallas_call(
        functools.partial(segment_kernel, z),
        out_shape=f32(m_rows, LANES),
        in_specs=[VM] * 5,
        out_specs=VM,
        compiler_params=params,
        name="segments",
    )(*x_coefs)
    maps = across_line(maps)

    values, tiles = pl.pallas_call(
        functools.partial(first_kernel, z),
        out_shape=[picked, tile_shape],
        in_specs=[VM] * 3,
        out_specs=[VM] * 2,
        scratch_shapes=[tile_mem, *gather_scratch(corners, fringe)],
        compiler_params=params,
        name="donors",
    )(donor_index, donor_weight, conserved)
    start = tiles

    for sweep in range(SUBITERS):
        last = sweep == SUBITERS - 1
        inbound = lax.all_to_all(values.reshape(devices, 4, LANES), ("line", "batch"), 0, 0, tiled=True)
        inbound = inbound.reshape(blocks * SUB, LANES)
        tiles, same_chip, next_chip = pl.pallas_call(
            functools.partial(place_kernel, z),
            out_shape=[tile_shape, f32(HALO * z.layer, LANES), f32(HALO * z.layer, LANES)],
            in_specs=[SM] + [VM] * 3,
            out_specs=[VM] * 3,
            scratch_shapes=[
                pltpu.VMEM((blocks, LANES), I32),
                pltpu.VMEM((blocks, LANES), I32),
                pltpu.SMEM((blocks, LANES), I32),
                pltpu.SMEM((blocks, LANES), I32),
                pltpu.SemaphoreType.DMA((2,)),
            ],
            compiler_params=params,
            name="receivers",
        )(place, receive, inbound, tiles)
        same_chip = lax.ppermute(same_chip, "line", [(i, i ^ 1) for i in range(count)])
        facing = [(i, i + 1) for i in range(1, count - 1, 2)]
        next_chip = lax.ppermute(next_chip, "line", facing + [(b, a) for a, b in facing])
        rhs, ends = pl.pallas_call(
            functools.partial(residual_kernel, z),
            out_shape=[f32(z.cl * z.layer, LANES), f32(s_rows, LANES)],
            in_specs=[SM] + [VM] * 12,
            out_specs=[VM] * 2,
            scratch_shapes=[tile_mem, pltpu.VMEM((z.layer, LANES), F32), inner_mem, spread_mem],
            compiler_params=params,
            name="residual",
        )(place, tiles, start, same_chip, next_chip, speed_xi, speed_eta, matrix, *x_coefs)
        ends = across_line(ends)
        scratch = [
            pltpu.VMEM((count * s_rows, LANES), F32),
            pltpu.VMEM((count * m_rows, LANES), F32),
            spread_mem,
            inner_mem,
            tile_mem,
        ]
        operands = (place, *ends, *maps, rhs, tiles, *x_coefs, *e_coefs)
        if last:
            return pl.pallas_call(
                functools.partial(solve_kernel, z, count, True),
                out_shape=f32(*conserved.shape),
                in_specs=[SM] + [VM] * (len(operands) - 1),
                out_specs=VM,
                scratch_shapes=scratch,
                compiler_params=params,
                name="solve_last",
            )(*operands)
        operands = (*operands, donor_index, donor_weight)
        values, tiles = pl.pallas_call(
            functools.partial(solve_kernel, z, count, False),
            out_shape=[picked, tile_shape],
            in_specs=[SM] + [VM] * (len(operands) - 1),
            out_specs=[VM] * 2,
            scratch_shapes=[*scratch, *gather_scratch(corners, fringe)],
            compiler_params=params,
            name="solve_donors",
        )(*operands)


def solution(mesh):
    field = P(None, "line", None, "batch")
    coef = P("line", None, "batch")
    fringe = ("line", "batch")
    in_specs = (field, P(), *[coef] * 12, P(None, fringe), P(None, fringe), P(fringe))
    return jax.shard_map(local, mesh=mesh, in_specs=in_specs, out_specs=field, check_vma=False)
```

```python
import functools

import jax
import jax.numpy as jnp
from jax import lax
from jax.experimental import pallas as pl
from jax.experimental.pallas import tpu as pltpu
from jax.sharding import PartitionSpec as P

SUBITERS = 2
DISSIP = 0.02
STEP = 0.1

SUB = 8
LANES = 128
HALO = 2
SLOTS = 4
GROUP = 2
MAPS = 12

VM = pl.BlockSpec(memory_space=pltpu.VMEM)
SM = pl.BlockSpec(memory_space=pltpu.SMEM)
F32 = jnp.float32
I32 = jnp.int32


def f32(*shape):
    return jax.ShapeDtypeStruct(shape, F32)


class Sizes:
    def __init__(self, fields, cl, ne, lb):
        assert fields <= SUB and ne == SUB and lb % LANES == 0
        self.fields, self.cl, self.ne, self.lb = fields, cl, ne, lb
        self.halves = lb // LANES
        self.columns = self.halves * ne
        self.layer = self.columns * SUB
        self.rows = (cl + 2 * HALO) * self.layer
        assert lb & (lb - 1) == 0

    def at(self, i, h, j):
        return ((i * self.halves + h) * SUB + j) * SUB

    def row_of_cell(self, cell):
        k_bits = self.lb.bit_length() - 1
        half = (cell & (self.lb - 1)) >> 7
        j = (cell >> k_bits) & (SUB - 1)
        i = cell >> (k_bits + 3)
        return ((i + HALO) * self.halves + half) * (SUB * SUB) + j * SUB


def grid_of(axis):
    return lax.broadcasted_iota(I32, (SUB, LANES), axis)


def swap_corners(block):
    keep = (grid_of(0) < 4) == (grid_of(1) < LANES // 2)
    return jnp.where(keep, block, pltpu.roll(pltpu.roll(block, 4, 0), LANES // 2, 1))


def total(parts):
    parts = list(parts)
    while len(parts) > 1:
        parts = [parts[i] + parts[i + 1] if i + 1 < len(parts) else parts[i] for i in range(0, len(parts), 2)]
    return parts[0]


def build_picks(k, block, donor, weight, picks):
    down = lax.broadcasted_iota(I32, (LANES, LANES), 0)
    base = pl.multiple_of(block * LANES, LANES)
    cell = donor[k : k + 1, pl.ds(base, LANES)] & (LANES - 1)
    chosen = jnp.where(down == cell, weight[k : k + 1, pl.ds(base, LANES)], 0.0)
    picks[k * LANES : (k + 1) * LANES, :] = chosen.T


def gather_block(corners, slots, block, tiles, out, picks, build_next):
    lane = grid_of(1)
    group = LANES // corners
    result = []
    for n in range(LANES):
        if n % group == 0:
            build_next(n // group)
        parts = []
        for k in range(corners):
            row = pl.multiple_of(slots[k, n], SUB)
            parts.append(tiles[pl.ds(row, SUB), :] * picks[k * LANES + n : k * LANES + n + 1, :])
        value = jnp.sum(total(parts), axis=1, keepdims=True)
        if n % 4 == 0:
            result.append(jnp.zeros((SUB, LANES), F32))
        result[-1] = jnp.where(lane == n, value, result[-1])
    out[pl.ds(pl.multiple_of(block * SUB, SUB), SUB), :] = swap_corners(total(result))


def gather_all(z, donor, weight, tiles, out, picks, where, slots, sems):
    corners = donor.shape[0]
    blocks = donor.shape[1] // LANES
    where[...] = z.row_of_cell(donor[...])

    def fetch(block, slot):
        source = where.at[:, pl.ds(pl.multiple_of(block * LANES, LANES), LANES)]
        return pltpu.make_async_copy(source, slots[slot], sems.at[slot])

    for slot in range(SLOTS):
        fetch(slot, slot).start()
    for k in range(corners):
        build_picks(k, 0, donor, weight, picks[0])

    def lap(turn, carry):
        for begin in range(0, SLOTS, GROUP):
            group = range(begin, begin + GROUP)
            for slot in group:
                fetch(SLOTS * turn + slot, slot).wait()
            for slot in group:
                block = SLOTS * turn + slot
                following = jnp.minimum(block + 1, blocks - 1)

                def build_next(k):
                    build_picks(k, following, donor, weight, picks[(slot + 1) % 2])

                gather_block(corners, slots[slot], block, tiles, out, picks[slot % 2], build_next)

            @pl.when(SLOTS * (turn + 1) < blocks)
            def _():
                for slot in group:
                    fetch(SLOTS * (turn + 1) + slot, slot).start()

        return carry

    lax.fori_loop(0, blocks // SLOTS, lap, 0)


def gather_scratch(corners, count):
    return [
        pltpu.VMEM((corners * LANES, LANES), F32),
        pltpu.VMEM((corners * LANES, LANES), F32),
        pltpu.VMEM((corners, count), I32),
        *[pltpu.SMEM((corners, LANES), I32) for _ in range(SLOTS)],
        pltpu.SemaphoreType.DMA((SLOTS,)),
    ]


def first_kernel(z, donor, weight, conserved, out, tiles_out, tiles, picks, picks_b, where, *rest):
    slots, sems = rest[:SLOTS], rest[SLOTS]
    tiles[...] = jnp.zeros(tiles.shape, F32)
    for f in range(z.fields):
        for i in range(z.cl):
            for h in range(z.halves):
                block = conserved[f, i, :, h * LANES : (h + 1) * LANES]
                tiles[pl.ds(z.at(i + HALO, h, 0) + f, SUB, stride=SUB), :] = block
    gather_all(z, donor, weight, tiles, out, (picks, picks_b), where, slots, sems)
    tiles_out[...] = tiles[...]


def place_kernel(z, place, receive, inbound, tiles, out, same_chip, next_chip, where, chosen, *rest):
    slots, sems = rest[:SLOTS], rest[SLOTS]
    blocks = receive.shape[0]
    lane = grid_of(1)
    cell = receive[...]
    where[pl.ds(0, blocks, stride=SUB), :] = z.row_of_cell(cell)

    def fetch(block, slot):
        source = where.at[pl.ds(pl.multiple_of(block * SUB, SUB), SUB), :]
        return pltpu.make_async_copy(source, slots[slot], sems.at[slot])

    for slot in range(SLOTS):
        fetch(slot, slot).start()
    out[...] = tiles[...]

    def lap(turn, carry):
        for slot in range(SLOTS):
            block = SLOTS * turn + slot
            values = swap_corners(inbound[pl.ds(pl.multiple_of(block * SUB, SUB), SUB), :])
            fetch(block, slot).wait()
            cell = receive[pl.ds(block, 1), :] & (LANES - 1)
            chosen[...] = jnp.where(lax.broadcasted_iota(I32, (LANES, LANES), 0) == cell, 1.0, 0.0).T
            for n in range(LANES):
                row = pl.multiple_of(slots[slot][0, n], SUB)
                mask = jnp.broadcast_to(chosen[n : n + 1, :], (SUB, LANES)) > 0.5
                column = jnp.sum(jnp.where(lane == n, values, 0.0), axis=1, keepdims=True)
                column = jnp.broadcast_to(column, (SUB, LANES))
                pltpu.store(out.at[pl.ds(row, SUB), :], column, mask=mask)

            @pl.when(block + SLOTS < blocks)
            def _():
                fetch(block + SLOTS, slot).start()

        return carry

    lax.fori_loop(0, blocks // SLOTS, lap, 0)
    core = place[1]
    low, high = HALO * z.layer, z.cl * z.layer
    same_chip[...] = out[pl.ds(pl.multiple_of(jnp.where(core == 0, high, low), SUB), HALO * z.layer), :]
    next_chip[...] = out[pl.ds(pl.multiple_of(jnp.where(core == 0, low, high), SUB), HALO * z.layer), :]


def line_of(ref, i, h, j):
    return ref[i, j : j + 1, h * LANES : (h + 1) * LANES]


def lower_at(z, rhs, low1, low2, dinv, keep, state, i, h, j):
    row = z.at(i, h, j)
    one, two = state
    inner, outer = rhs
    if i < HALO:
        right = outer[row : row + SUB, :]
    elif i < z.cl - HALO:
        right = inner[row - HALO * z.layer : row - HALO * z.layer + SUB, :]
    else:
        skip = (z.cl - 2 * HALO) * z.layer
        right = outer[row - skip : row - skip + SUB, :]
    new = line_of(dinv, i, h, j) * (
        right - line_of(low1, i, h, j) * one - line_of(low2, i, h, j) * two
    )
    keep[row : row + SUB, :] = new
    return (new, one)


def upper_at(z, keep, up1, up2, state, i, h, j):
    row = z.at(i, h, j)
    one, two = state
    new = keep[row : row + SUB, :] - line_of(up1, i, h, j) * one - line_of(up2, i, h, j) * two
    return (new, one)


def segment_kernel(z, low1, low2, dinv, up1, up2, out):
    for h in range(z.halves):
        cut = slice(h * LANES, (h + 1) * LANES)
        zero, one = jnp.zeros((SUB, LANES), F32), jnp.ones((SUB, LANES), F32)
        planes = [None] * MAPS
        for unit in range(2):
            a, b = (one, zero) if unit == 0 else (zero, one)
            kept = []
            for i in range(z.cl):
                a, b = -dinv[i, :, cut] * (low1[i, :, cut] * a + low2[i, :, cut] * b), a
                kept.append(a)
            planes[unit], planes[2 + unit] = a, b
            a, b = zero, zero
            for i in reversed(range(z.cl)):
                a, b = kept[i] - up1[i, :, cut] * a - up2[i, :, cut] * b, a
            planes[4 + unit], planes[6 + unit] = a, b
            a, b = (one, zero) if unit == 0 else (zero, one)
            for i in reversed(range(z.cl)):
                a, b = -up1[i, :, cut] * a - up2[i, :, cut] * b, a
            planes[8 + unit], planes[10 + unit] = a, b
        for p in range(12):
            row = (h * MAPS + p) * SUB
            out[row : row + SUB, :] = planes[p]


def compose_kernel(z, with_maps, place, own, other, own_maps, other_maps, *outs):
    chip, half = outs[0], outs[-1]
    first = place[1] == 0

    def pick(left, mine, theirs, row):
        block = mine[row : row + SUB, :], theirs[row : row + SUB, :]
        return jnp.where(first == left, *block)

    for h in range(z.halves):
        l = [pick(True, own_maps, other_maps, (h * MAPS + p) * SUB) for p in range(MAPS)]
        r = [pick(False, own_maps, other_maps, (h * MAPS + p) * SUB) for p in range(MAPS)]
        for f in range(z.fields):
            rows = [((h * z.fields + f) * 4 + v) * SUB for v in range(4)]
            a, b, g, k = [pick(True, own, other, row) for row in rows]
            c, d, m, n = [pick(False, own, other, row) for row in rows]
            c = c + r[0] * a + r[1] * b
            d = d + r[2] * a + r[3] * b
            m = m + r[4] * a + r[5] * b
            n = n + r[6] * a + r[7] * b
            g = g + l[8] * m + l[9] * n
            k = k + l[10] * m + l[11] * n
            for row, value in zip(rows, (c, d, g, k)):
                chip[row : row + SUB, :] = value
        if with_maps:
            t = [r[4] * l[0] + r[5] * l[2], r[4] * l[1] + r[5] * l[3]]
            t += [r[6] * l[0] + r[7] * l[2], r[6] * l[1] + r[7] * l[3]]
            both = [
                r[0] * l[0] + r[1] * l[2],
                r[0] * l[1] + r[1] * l[3],
                r[2] * l[0] + r[3] * l[2],
                r[2] * l[1] + r[3] * l[3],
                l[4] + l[8] * t[0] + l[9] * t[2],
                l[5] + l[8] * t[1] + l[9] * t[3],
                l[6] + l[10] * t[0] + l[11] * t[2],
                l[7] + l[10] * t[1] + l[11] * t[3],
                l[8] * r[8] + l[9] * r[10],
                l[8] * r[9] + l[9] * r[11],
                l[10] * r[8] + l[11] * r[10],
                l[10] * r[9] + l[11] * r[11],
            ]
            for p in range(MAPS):
                row = (h * MAPS + p) * SUB
                outs[1][row : row + SUB, :] = both[p]
    ends, maps = z.fields * 4 * SUB, MAPS * SUB
    half[0:ends, :] = chip[pl.ds(pl.multiple_of(place[1] * ends, SUB), ends), :]
    if with_maps:
        half[ends : ends + maps, :] = outs[1][pl.ds(pl.multiple_of(place[1] * maps, SUB), maps), :]


def flux_columns(z, matrix):
    return [jnp.broadcast_to(matrix[:, d : d + 1] * (-0.5 * STEP), (SUB, LANES)) for d in range(z.fields)]


def residual_layer(z, i, field, at, start, speed_xi, speed_eta, columns, slope, rhs, to):
    nothing = jnp.zeros((SUB, LANES), F32)

    def point(step, h, j):
        if j < 0 or j >= SUB:
            return nothing
        return field[pl.ds(at + step * z.layer + z.at(0, h, j), SUB), :]

    for h in range(z.halves):
        for j in range(SUB):
            row = z.at(0, h, j)
            centre = point(0, h, j)
            before, after = point(-1, h, j), point(1, h, j)
            under, over = point(0, h, j - 1), point(0, h, j + 1)
            change = line_of(speed_xi, i, h, j) * (after - before) + line_of(speed_eta, i, h, j) * (over - under)
            slope[row : row + SUB, :] = change
            near = (before + after) + (under + over)
            far = (point(-2, h, j) + point(2, h, j)) + (point(0, h, j - 2) + point(0, h, j + 2))
            fourth = far - 4.0 * near + 12.0 * centre
            value = -(STEP * DISSIP) * fourth - STEP * (centre - start[pl.ds((i + HALO) * z.layer + row, SUB), :])
            value = value + total([columns[d] * slope[row + d : row + d + 1, :] for d in range(z.fields)])
            rhs[pl.ds(to + row, SUB), :] = value


def interior_kernel(z, tiles, start, speed_xi, speed_eta, matrix, rhs, slope):
    columns = flux_columns(z, matrix)

    def layer(n, carry):
        at = pl.multiple_of((n + 2 * HALO) * z.layer, SUB)
        to = pl.multiple_of(n * z.layer, SUB)
        residual_layer(z, n + HALO, tiles, at, start, speed_xi, speed_eta, columns, slope, rhs, to)
        return carry

    lax.fori_loop(0, z.cl - 2 * HALO, layer, 0)


def edges_kernel(
    z, place, tiles, start, same_chip, next_chip, speed_xi, speed_eta, matrix,
    low1, low2, dinv, up1, up2, inner, outer, ends, low, high, slope, keep, spread,
):
    first = place[1] == 0
    edge, wide = HALO * z.layer, 2 * HALO * z.layer
    low[0:edge, :] = jnp.where(first, next_chip[...], same_chip[...])
    low[edge : edge + wide, :] = tiles[edge : edge + wide, :]
    high[wide : wide + edge, :] = jnp.where(first, same_chip[...], next_chip[...])
    high[0:wide, :] = tiles[z.rows - edge - wide : z.rows - edge, :]
    columns = flux_columns(z, matrix)
    for n in range(HALO):
        at, to = (n + HALO) * z.layer, n * z.layer
        residual_layer(z, n, low, at, start, speed_xi, speed_eta, columns, slope, outer, to)
        i = z.cl - HALO + n
        residual_layer(z, i, high, at, start, speed_xi, speed_eta, columns, slope, outer, edge + to)
    nothing = jnp.zeros((SUB, LANES), F32)
    for h in range(z.halves):
        states = [(nothing, nothing)] * SUB
        for i in range(z.cl):
            states = [lower_at(z, (inner, outer), low1, low2, dinv, keep, states[j], i, h, j) for j in range(SUB)]
        lowered = states
        states = [(nothing, nothing)] * SUB
        for i in reversed(range(z.cl)):
            states = [upper_at(z, keep, up1, up2, states[j], i, h, j) for j in range(SUB)]
        for j in range(SUB):
            for v, value in enumerate((*lowered[j], *states[j])):
                spread[pl.ds((h * SUB * 4 + v) * SUB + j, SUB, stride=4 * SUB), :] = value
        size = z.fields * 4 * SUB
        ends[h * size : (h + 1) * size, :] = spread[h * SUB * 4 * SUB : h * SUB * 4 * SUB + size, :]


def solve_kernel(z, chips, last, *refs):
    place, refs = refs[0], refs[1:]
    own, other, own_maps, other_maps, chip_ends, chip_maps = refs[:6]
    far, far_maps, refs = refs[6 : 4 + 2 * chips], refs[4 + 2 * chips : 2 + 4 * chips], refs[2 + 4 * chips :]
    rhs, refs = refs[:2], refs[2:]
    (tiles, low1, low2, dinv, up1, up2, e_low1, e_low2, e_dinv, e_up1, e_up2), refs = refs[:11], refs[11:]
    if last:
        out, states, planes, spread, keep, fresh = refs
    else:
        donor, weight, out, tiles_out, states, planes, spread, keep, fresh, picks, picks_b, where, *rest = refs
    core, chip = place[1], place[2]
    first = core == 0
    s_rows, m_rows = z.fields * 4 * SUB, MAPS * SUB

    def put(ref, at_chip, half, rows, source, begin):
        at = (at_chip * z.halves + half) * rows
        ref[pl.ds(pl.multiple_of(at, SUB), rows), :] = source[begin : begin + rows, :]

    for half in range(z.halves):
        put(states, chip, half, s_rows, chip_ends, half * s_rows)
        put(planes, chip, half, m_rows, chip_maps, half * m_rows)
    for s in range(1, chips):
        for t in range(2):
            put(states, chip ^ s, core ^ t, s_rows, far[2 * (s - 1) + t], 0)
            put(planes, chip ^ s, core ^ t, m_rows, far_maps[2 * (s - 1) + t], s_rows)

    zero = jnp.zeros((SUB, LANES), F32)
    for h in range(z.halves):

        def plane(at, p):
            row = ((at * z.halves + h) * MAPS + p) * SUB
            return planes[row : row + SUB, :]

        def end(at, f, v):
            row = ((at * z.halves + h) * z.fields * 4 + f * 4 + v) * SUB
            return states[row : row + SUB, :]

        entering = [[(zero, zero)] for _ in range(z.fields)]
        for d in range(chips - 1):
            for f in range(z.fields):
                a, b = entering[f][-1]
                entering[f].append(
                    (
                        end(d, f, 0) + plane(d, 0) * a + plane(d, 1) * b,
                        end(d, f, 1) + plane(d, 2) * a + plane(d, 3) * b,
                    )
                )
        mine = [[zero] * 4 for _ in range(z.fields)]
        returning = [(zero, zero)] * z.fields
        for d in reversed(range(chips)):
            for f in range(z.fields):
                a, b = entering[f][d]
                g, k = returning[f]
                mine[f] = [jnp.where(chip == d, new, old) for new, old in zip((a, b, g, k), mine[f])]
                returning[f] = (
                    (end(d, f, 2) + plane(d, 4) * a + plane(d, 5) * b) + (plane(d, 8) * g + plane(d, 9) * k),
                    (end(d, f, 3) + plane(d, 6) * a + plane(d, 7) * b) + (plane(d, 10) * g + plane(d, 11) * k),
                )

        def pick(left, one, two, row):
            return jnp.where(first == left, one[row : row + SUB, :], two[row : row + SUB, :])

        l = [pick(True, own_maps, other_maps, (h * MAPS + p) * SUB) for p in range(4)]
        r = [pick(False, own_maps, other_maps, (h * MAPS + p) * SUB) for p in range(MAPS)]
        for f in range(SUB):
            at = h * SUB * 4 + f * 4
            if f < z.fields:
                a, b, g, k = mine[f]
                rows = [((h * z.fields + f) * 4 + v) * SUB for v in range(4)]
                c = pick(True, own, other, rows[0]) + l[0] * a + l[1] * b
                d = pick(True, own, other, rows[1]) + l[2] * a + l[3] * b
                m = (pick(False, own, other, rows[2]) + r[4] * c + r[5] * d) + (r[8] * g + r[9] * k)
                n = (pick(False, own, other, rows[3]) + r[6] * c + r[7] * d) + (r[10] * g + r[11] * k)
                values = [jnp.where(first, a, c), jnp.where(first, b, d), jnp.where(first, m, g), jnp.where(first, n, k)]
            else:
                values = [zero] * 4
            for v in range(4):
                spread[(at + v) * SUB : (at + v + 1) * SUB, :] = values[v]

    def enter(v, h, j):
        return spread[pl.ds((h * SUB * 4 + v) * SUB + j, SUB, stride=4 * SUB), :]

    if not last:
        fresh[0 : HALO * z.layer, :] = jnp.zeros((HALO * z.layer, LANES), F32)
        fresh[z.rows - HALO * z.layer : z.rows, :] = jnp.zeros((HALO * z.layer, LANES), F32)
    for h in range(z.halves):
        state = [(enter(0, h, j), enter(1, h, j)) for j in range(SUB)]
        for i in range(z.cl):
            state = [lower_at(z, rhs, low1, low2, dinv, keep, state[j], i, h, j) for j in range(SUB)]
        state = [(enter(2, h, j), enter(3, h, j)) for j in range(SUB)]
        for i in reversed(range(z.cl)):
            state = [upper_at(z, keep, up1, up2, state[j], i, h, j) for j in range(SUB)]
            one, two = zero, zero
            lowered = []
            for j in range(SUB):
                new = line_of(e_dinv, i, h, j) * (
                    state[j][0] - line_of(e_low1, i, h, j) * one - line_of(e_low2, i, h, j) * two
                )
                one, two = new, one
                lowered.append(new)
            one, two = zero, zero
            for j in reversed(range(SUB)):
                new = lowered[j] - line_of(e_up1, i, h, j) * one - line_of(e_up2, i, h, j) * two
                one, two = new, one
                row = z.at(i + HALO, h, j)
                fresh[row : row + SUB, :] = tiles[row : row + SUB, :] + new
    if last:
        for f in range(z.fields):
            for i in range(z.cl):
                for h in range(z.halves):
                    out[f, i, :, h * LANES : (h + 1) * LANES] = fresh[
                        pl.ds(z.at(i + HALO, h, 0) + f, SUB, stride=SUB), :
                    ]
    else:
        tiles_out[...] = fresh[...]
        gather_all(z, donor, weight, fresh, out, (picks, picks_b), where, rest[:SLOTS], rest[SLOTS])


def to_other_core(array):
    return lax.ppermute(array, "line", [(i, i ^ 1) for i in range(lax.axis_size("line"))])


def from_other_chips(array):
    size = lax.axis_size("line")
    result = []
    for s in range(1, size // 2):
        there = lax.ppermute(array, "line", [(i, i ^ (2 * s)) for i in range(size)])
        result += [there, to_other_core(there)]
    return result


def local(
    conserved, flux_matrix, speed_xi, speed_eta, x_low1, x_low2, x_dinv, x_up1, x_up2,
    e_low1, e_low2, e_dinv, e_up1, e_up2, donor_index, donor_weight, receive_index,
):
    z = Sizes(*conserved.shape)
    count = lax.axis_size("line")
    devices = count * lax.axis_size("batch")
    corners, fringe = donor_index.shape
    assert fringe == devices * (LANES // 2) and count % 2 == 0 and count & (count - 1) == 0
    blocks = fringe // LANES
    me = lax.axis_index("line").astype(I32)
    place = jnp.stack([me, me & 1, me >> 1])
    matrix = jnp.pad(flux_matrix, ((0, SUB - z.fields), (0, LANES - z.fields)))
    receive = receive_index.reshape(blocks, LANES)
    x_coefs = (x_low1, x_low2, x_dinv, x_up1, x_up2)
    e_coefs = (e_low1, e_low2, e_dinv, e_up1, e_up2)
    params = pltpu.CompilerParams(vmem_limit_bytes=32 * 1024 * 1024)
    picked = f32(blocks * SUB, LANES)
    tile_shape = f32(z.rows, LANES)
    tile_mem = pltpu.VMEM((z.rows, LANES), F32)
    inner_mem = pltpu.VMEM((z.cl * z.layer, LANES), F32)
    spread_mem = pltpu.VMEM((SUB * 4 * z.columns, LANES), F32)
    s_rows, m_rows = z.fields * 4 * SUB, MAPS * SUB
    chips = count // 2
    assert z.halves == 2

    maps = pl.pallas_call(
        functools.partial(segment_kernel, z),
        out_shape=f32(z.halves * m_rows, LANES),
        in_specs=[VM] * 5,
        out_specs=VM,
        compiler_params=params,
        name="segments",
    )(*x_coefs)
    other_maps = to_other_core(maps)

    values, tiles = pl.pallas_call(
        functools.partial(first_kernel, z),
        out_shape=[picked, tile_shape],
        in_specs=[VM] * 3,
        out_specs=[VM] * 2,
        scratch_shapes=[tile_mem, *gather_scratch(corners, fringe)],
        compiler_params=params,
        name="donors",
    )(donor_index, donor_weight, conserved)
    start = tiles

    for sweep in range(SUBITERS):
        last = sweep == SUBITERS - 1
        inbound = lax.all_to_all(values.reshape(devices, 4, LANES), ("line", "batch"), 0, 0, tiled=True)
        inbound = inbound.reshape(blocks * SUB, LANES)
        tiles, same_chip, next_chip = pl.pallas_call(
            functools.partial(place_kernel, z),
            out_shape=[tile_shape, f32(HALO * z.layer, LANES), f32(HALO * z.layer, LANES)],
            in_specs=[SM] + [VM] * 3,
            out_specs=[VM] * 3,
            scratch_shapes=[
                pltpu.VMEM((blocks * SUB, LANES), I32),
                pltpu.VMEM((LANES, LANES), F32),
                *[pltpu.SMEM((SUB, LANES), I32) for _ in range(SLOTS)],
                pltpu.SemaphoreType.DMA((SLOTS,)),
            ],
            compiler_params=params,
            name="receivers",
        )(place, receive, inbound, tiles)
        same_chip = lax.ppermute(same_chip, "line", [(i, i ^ 1) for i in range(count)])
        facing = [(i, i + 1) for i in range(1, count - 1, 2)]
        next_chip = lax.ppermute(next_chip, "line", facing + [(b, a) for a, b in facing])
        layers = z.cl - 2 * HALO
        inner = pl.pallas_call(
            functools.partial(interior_kernel, z),
            out_shape=f32(layers * z.layer, LANES),
            in_specs=[VM] * 5,
            out_specs=VM,
            scratch_shapes=[pltpu.VMEM((z.layer, LANES), F32)],
            compiler_params=params,
            cost_estimate=pl.CostEstimate(
                flops=layers * z.layer * LANES * 40, bytes_accessed=layers * z.layer * LANES * 16, transcendentals=0
            ),
            name="interior",
        )(tiles, start, speed_xi, speed_eta, matrix)
        outer, ends = pl.pallas_call(
            functools.partial(edges_kernel, z),
            out_shape=[f32(2 * HALO * z.layer, LANES), f32(z.halves * s_rows, LANES)],
            in_specs=[SM] + [VM] * 13,
            out_specs=[VM] * 2,
            scratch_shapes=[
                pltpu.VMEM((3 * HALO * z.layer, LANES), F32),
                pltpu.VMEM((3 * HALO * z.layer, LANES), F32),
                pltpu.VMEM((z.layer, LANES), F32),
                inner_mem,
                spread_mem,
            ],
            compiler_params=params,
            name="edges",
        )(place, tiles, start, same_chip, next_chip, speed_xi, speed_eta, matrix, *x_coefs, inner)
        other_ends = to_other_core(ends)
        with_maps = sweep == 0
        shapes = [f32(z.halves * s_rows, LANES)]
        if with_maps:
            shapes.append(f32(z.halves * m_rows, LANES))
        shapes.append(f32(s_rows + m_rows * with_maps, LANES))
        composed = pl.pallas_call(
            functools.partial(compose_kernel, z, with_maps),
            out_shape=shapes,
            in_specs=[SM] + [VM] * 4,
            out_specs=[VM] * len(shapes),
            compiler_params=params,
            name="compose",
        )(place, ends, other_ends, maps, other_maps)
        chip_ends, half = composed[0], composed[-1]
        far = from_other_chips(half)
        if with_maps:
            chip_maps, far_maps = composed[1], far
        scratch = [
            pltpu.VMEM((chips * z.halves * s_rows, LANES), F32),
            pltpu.VMEM((chips * z.halves * m_rows, LANES), F32),
            spread_mem,
            inner_mem,
            tile_mem,
        ]
        operands = (place, ends, other_ends, maps, other_maps, chip_ends, chip_maps, *far, *far_maps)
        operands = (*operands, inner, outer, tiles, *x_coefs, *e_coefs)
        if last:
            return pl.pallas_call(
                functools.partial(solve_kernel, z, chips, True),
                out_shape=f32(*conserved.shape),
                in_specs=[SM] + [VM] * (len(operands) - 1),
                out_specs=VM,
                scratch_shapes=scratch,
                compiler_params=params,
                name="solve_last",
            )(*operands)
        operands = (*operands, donor_index, donor_weight)
        values, tiles = pl.pallas_call(
            functools.partial(solve_kernel, z, chips, False),
            out_shape=[picked, tile_shape],
            in_specs=[SM] + [VM] * (len(operands) - 1),
            out_specs=[VM] * 2,
            scratch_shapes=[*scratch, *gather_scratch(corners, fringe)],
            compiler_params=params,
            name="solve_donors",
        )(*operands)


def solution(mesh):
    field = P(None, "line", None, "batch")
    coef = P("line", None, "batch")
    fringe = ("line", "batch")
    in_specs = (field, P(), *[coef] * 12, P(None, fringe), P(None, fringe), P(fringe))
    return jax.shard_map(local, mesh=mesh, in_specs=in_specs, out_specs=field, check_vma=False)
```

```python
import functools

import jax
import jax.numpy as jnp
from jax import lax
from jax.experimental import pallas as pl
from jax.experimental.pallas import tpu as pltpu
from jax.sharding import PartitionSpec as P

SUBITERS = 2
DISSIP = 0.02
STEP = 0.1

SUB = 8
LANES = 128
HALO = 2
SLOTS = 4
GROUP = 2
MAPS = 12

VM = pl.BlockSpec(memory_space=pltpu.VMEM)
SM = pl.BlockSpec(memory_space=pltpu.SMEM)
F32 = jnp.float32
I32 = jnp.int32


def f32(*shape):
    return jax.ShapeDtypeStruct(shape, F32)


class Sizes:
    def __init__(self, fields, cl, ne, lb):
        assert fields <= SUB and ne == SUB and lb % LANES == 0
        self.fields, self.cl, self.ne, self.lb = fields, cl, ne, lb
        self.halves = lb // LANES
        self.columns = self.halves * ne
        self.layer = self.columns * SUB
        self.rows = (cl + 2 * HALO) * self.layer
        assert lb & (lb - 1) == 0

    def at(self, i, h, j):
        return ((i * self.halves + h) * SUB + j) * SUB

    def row_of_cell(self, cell):
        k_bits = self.lb.bit_length() - 1
        half = (cell & (self.lb - 1)) >> 7
        j = (cell >> k_bits) & (SUB - 1)
        i = cell >> (k_bits + 3)
        return ((i + HALO) * self.halves + half) * (SUB * SUB) + j * SUB


def grid_of(axis):
    return lax.broadcasted_iota(I32, (SUB, LANES), axis)


def swap_corners(block):
    keep = (grid_of(0) < 4) == (grid_of(1) < LANES // 2)
    return jnp.where(keep, block, pltpu.roll(pltpu.roll(block, 4, 0), LANES // 2, 1))


def total(parts):
    parts = list(parts)
    while len(parts) > 1:
        parts = [parts[i] + parts[i + 1] if i + 1 < len(parts) else parts[i] for i in range(0, len(parts), 2)]
    return parts[0]


def build_picks(k, block, donor, weight, picks):
    down = lax.broadcasted_iota(I32, (LANES, LANES), 0)
    base = pl.multiple_of(block * LANES, LANES)
    cell = donor[k : k + 1, pl.ds(base, LANES)] & (LANES - 1)
    chosen = jnp.where(down == cell, weight[k : k + 1, pl.ds(base, LANES)], 0.0)
    picks[k * LANES : (k + 1) * LANES, :] = chosen.T


def gather_block(corners, slots, block, tiles, out, picks, build_next):
    lane = grid_of(1)
    group = LANES // corners
    result = []
    for n in range(LANES):
        if n % group == 0:
            build_next(n // group)
        parts = []
        for k in range(corners):
            row = pl.multiple_of(slots[k, n], SUB)
            parts.append(tiles[pl.ds(row, SUB), :] * picks[k * LANES + n : k * LANES + n + 1, :])
        value = jnp.sum(total(parts), axis=1, keepdims=True)
        if n % 4 == 0:
            result.append(jnp.zeros((SUB, LANES), F32))
        result[-1] = jnp.where(lane == n, value, result[-1])
    out[pl.ds(pl.multiple_of(block * SUB, SUB), SUB), :] = swap_corners(total(result))


def gather_all(z, donor, weight, tiles, out, picks, where, slots, sems):
    corners = donor.shape[0]
    blocks = donor.shape[1] // LANES
    where[...] = z.row_of_cell(donor[...])

    def fetch(block, slot):
        source = where.at[:, pl.ds(pl.multiple_of(block * LANES, LANES), LANES)]
        return pltpu.make_async_copy(source, slots[slot], sems.at[slot])

    for slot in range(SLOTS):
        fetch(slot, slot).start()
    for k in range(corners):
        build_picks(k, 0, donor, weight, picks[0])

    def lap(turn, carry):
        for begin in range(0, SLOTS, GROUP):
            group = range(begin, begin + GROUP)
            for slot in group:
                fetch(SLOTS * turn + slot, slot).wait()
            for slot in group:
                block = SLOTS * turn + slot
                following = jnp.minimum(block + 1, blocks - 1)

                def build_next(k):
                    build_picks(k, following, donor, weight, picks[(slot + 1) % 2])

                gather_block(corners, slots[slot], block, tiles, out, picks[slot % 2], build_next)

            @pl.when(SLOTS * (turn + 1) < blocks)
            def _():
                for slot in group:
                    fetch(SLOTS * (turn + 1) + slot, slot).start()

        return carry

    lax.fori_loop(0, blocks // SLOTS, lap, 0)


def gather_scratch(corners, count):
    return [
        pltpu.VMEM((corners * LANES, LANES), F32),
        pltpu.VMEM((corners * LANES, LANES), F32),
        pltpu.VMEM((corners, count), I32),
        *[pltpu.SMEM((corners, LANES), I32) for _ in range(SLOTS)],
        pltpu.SemaphoreType.DMA((SLOTS,)),
    ]


def first_kernel(z, donor, weight, conserved, out, tiles_out, tiles, picks, picks_b, where, *rest):
    slots, sems = rest[:SLOTS], rest[SLOTS]
    tiles[...] = jnp.zeros(tiles.shape, F32)
    for f in range(z.fields):
        for i in range(z.cl):
            for h in range(z.halves):
                block = conserved[f, i, :, h * LANES : (h + 1) * LANES]
                tiles[pl.ds(z.at(i + HALO, h, 0) + f, SUB, stride=SUB), :] = block
    gather_all(z, donor, weight, tiles, out, (picks, picks_b), where, slots, sems)
    tiles_out[...] = tiles[...]


def place_kernel(z, place, receive, inbound, tiles, out, same_chip, next_chip, where, chosen, *rest):
    slots, sems = rest[:SLOTS], rest[SLOTS]
    blocks = receive.shape[0]
    lane = grid_of(1)
    cell = receive[...]
    where[pl.ds(0, blocks, stride=SUB), :] = z.row_of_cell(cell)
    where[pl.ds(1, blocks, stride=SUB), :] = (cell - lax.broadcasted_iota(I32, (blocks, LANES), 1)) & (LANES - 1)

    def fetch(block, slot):
        source = where.at[pl.ds(pl.multiple_of(block * SUB, SUB), SUB), :]
        return pltpu.make_async_copy(source, slots[slot], sems.at[slot])

    for slot in range(SLOTS):
        fetch(slot, slot).start()
    out[...] = tiles[...]

    def lap(turn, carry):
        for begin in range(0, SLOTS, GROUP):
            group = range(begin, begin + GROUP)
            for slot in group:
                fetch(SLOTS * turn + slot, slot).wait()
            for slot in group:
                cell = receive[pl.ds(SLOTS * turn + slot, 1), :] & (LANES - 1)
                down = lax.broadcasted_iota(I32, (LANES, LANES), 0)
                chosen[slot * LANES : (slot + 1) * LANES, :] = jnp.where(down == cell, 1.0, 0.0).T
            for slot in group:
                at = pl.multiple_of((SLOTS * turn + slot) * SUB, SUB)
                values = swap_corners(inbound[pl.ds(at, SUB), :])
                for n in range(LANES):
                    row = pl.multiple_of(slots[slot][0, n], SUB)
                    pick = chosen[slot * LANES + n : slot * LANES + n + 1, :]
                    mask = jnp.broadcast_to(pick, (SUB, LANES)) > 0.5
                    column = jnp.sum(jnp.where(lane == n, values, 0.0), axis=1, keepdims=True)
                    column = jnp.broadcast_to(column, (SUB, LANES))
                    pltpu.store(out.at[pl.ds(row, SUB), :], column, mask=mask)

            @pl.when(SLOTS * (turn + 1) < blocks)
            def _():
                for slot in group:
                    fetch(SLOTS * (turn + 1) + slot, slot).start()

        return carry

    lax.fori_loop(0, blocks // SLOTS, lap, 0)
    core = place[1]
    low, high = HALO * z.layer, z.cl * z.layer
    same_chip[...] = out[pl.ds(pl.multiple_of(jnp.where(core == 0, high, low), SUB), HALO * z.layer), :]
    next_chip[...] = out[pl.ds(pl.multiple_of(jnp.where(core == 0, low, high), SUB), HALO * z.layer), :]


def line_of(ref, i, h, j):
    return ref[i, j : j + 1, h * LANES : (h + 1) * LANES]


def lower_at(z, rhs, low1, low2, dinv, keep, state, i, h, j):
    row = z.at(i, h, j)
    one, two = state
    inner, outer = rhs
    if i < HALO:
        right = outer[row : row + SUB, :]
    elif i < z.cl - HALO:
        right = inner[row - HALO * z.layer : row - HALO * z.layer + SUB, :]
    else:
        skip = (z.cl - 2 * HALO) * z.layer
        right = outer[row - skip : row - skip + SUB, :]
    new = line_of(dinv, i, h, j) * (
        right - line_of(low1, i, h, j) * one - line_of(low2, i, h, j) * two
    )
    keep[row : row + SUB, :] = new
    return (new, one)


def upper_at(z, keep, up1, up2, state, i, h, j):
    row = z.at(i, h, j)
    one, two = state
    new = keep[row : row + SUB, :] - line_of(up1, i, h, j) * one - line_of(up2, i, h, j) * two
    return (new, one)


def segment_kernel(z, low1, low2, dinv, up1, up2, out):
    for h in range(z.halves):
        cut = slice(h * LANES, (h + 1) * LANES)
        zero, one = jnp.zeros((SUB, LANES), F32), jnp.ones((SUB, LANES), F32)
        planes = [None] * MAPS
        for unit in range(2):
            a, b = (one, zero) if unit == 0 else (zero, one)
            kept = []
            for i in range(z.cl):
                a, b = -dinv[i, :, cut] * (low1[i, :, cut] * a + low2[i, :, cut] * b), a
                kept.append(a)
            planes[unit], planes[2 + unit] = a, b
            a, b = zero, zero
            for i in reversed(range(z.cl)):
                a, b = kept[i] - up1[i, :, cut] * a - up2[i, :, cut] * b, a
            planes[4 + unit], planes[6 + unit] = a, b
            a, b = (one, zero) if unit == 0 else (zero, one)
            for i in reversed(range(z.cl)):
                a, b = -up1[i, :, cut] * a - up2[i, :, cut] * b, a
            planes[8 + unit], planes[10 + unit] = a, b
        for p in range(12):
            row = (h * MAPS + p) * SUB
            out[row : row + SUB, :] = planes[p]


def compose_kernel(z, with_maps, place, own, other, own_maps, other_maps, *outs):
    chip, half = outs[0], outs[-1]
    first = place[1] == 0

    def pick(left, mine, theirs, row):
        block = mine[row : row + SUB, :], theirs[row : row + SUB, :]
        return jnp.where(first == left, *block)

    for h in range(z.halves):
        l = [pick(True, own_maps, other_maps, (h * MAPS + p) * SUB) for p in range(MAPS)]
        r = [pick(False, own_maps, other_maps, (h * MAPS + p) * SUB) for p in range(MAPS)]
        for f in range(z.fields):
            rows = [((h * z.fields + f) * 4 + v) * SUB for v in range(4)]
            a, b, g, k = [pick(True, own, other, row) for row in rows]
            c, d, m, n = [pick(False, own, other, row) for row in rows]
            c = c + r[0] * a + r[1] * b
            d = d + r[2] * a + r[3] * b
            m = m + r[4] * a + r[5] * b
            n = n + r[6] * a + r[7] * b
            g = g + l[8] * m + l[9] * n
            k = k + l[10] * m + l[11] * n
            for row, value in zip(rows, (c, d, g, k)):
                chip[row : row + SUB, :] = value
        if with_maps:
            t = [r[4] * l[0] + r[5] * l[2], r[4] * l[1] + r[5] * l[3]]
            t += [r[6] * l[0] + r[7] * l[2], r[6] * l[1] + r[7] * l[3]]
            both = [
                r[0] * l[0] + r[1] * l[2],
                r[0] * l[1] + r[1] * l[3],
                r[2] * l[0] + r[3] * l[2],
                r[2] * l[1] + r[3] * l[3],
                l[4] + l[8] * t[0] + l[9] * t[2],
                l[5] + l[8] * t[1] + l[9] * t[3],
                l[6] + l[10] * t[0] + l[11] * t[2],
                l[7] + l[10] * t[1] + l[11] * t[3],
                l[8] * r[8] + l[9] * r[10],
                l[8] * r[9] + l[9] * r[11],
                l[10] * r[8] + l[11] * r[10],
                l[10] * r[9] + l[11] * r[11],
            ]
            for p in range(MAPS):
                row = (h * MAPS + p) * SUB
                outs[1][row : row + SUB, :] = both[p]
    ends, maps = z.fields * 4 * SUB, MAPS * SUB
    half[0:ends, :] = chip[pl.ds(pl.multiple_of(place[1] * ends, SUB), ends), :]
    if with_maps:
        half[ends : ends + maps, :] = outs[1][pl.ds(pl.multiple_of(place[1] * maps, SUB), maps), :]


def flux_columns(z, matrix):
    return [jnp.broadcast_to(matrix[:, d : d + 1] * (-0.5 * STEP), (SUB, LANES)) for d in range(z.fields)]


def residual_layer(z, i, field, at, start, speed_xi, speed_eta, columns, slope, rhs, to):
    nothing = jnp.zeros((SUB, LANES), F32)

    def point(step, h, j):
        if j < 0 or j >= SUB:
            return nothing
        return field[pl.ds(at + step * z.layer + z.at(0, h, j), SUB), :]

    for h in range(z.halves):
        for j in range(SUB):
            row = z.at(0, h, j)
            centre = point(0, h, j)
            before, after = point(-1, h, j), point(1, h, j)
            under, over = point(0, h, j - 1), point(0, h, j + 1)
            change = line_of(speed_xi, i, h, j) * (after - before) + line_of(speed_eta, i, h, j) * (over - under)
            slope[row : row + SUB, :] = change
            near = (before + after) + (under + over)
            far = (point(-2, h, j) + point(2, h, j)) + (point(0, h, j - 2) + point(0, h, j + 2))
            fourth = far - 4.0 * near + 12.0 * centre
            value = -(STEP * DISSIP) * fourth - STEP * (centre - start[pl.ds((i + HALO) * z.layer + row, SUB), :])
            value = value + total([columns[d] * slope[row + d : row + d + 1, :] for d in range(z.fields)])
            rhs[pl.ds(to + row, SUB), :] = value


def interior_kernel(z, tiles, start, speed_xi, speed_eta, matrix, rhs, slope):
    columns = flux_columns(z, matrix)

    def layer(n, carry):
        at = pl.multiple_of((n + 2 * HALO) * z.layer, SUB)
        to = pl.multiple_of(n * z.layer, SUB)
        residual_layer(z, n + HALO, tiles, at, start, speed_xi, speed_eta, columns, slope, rhs, to)
        return carry

    lax.fori_loop(0, z.cl - 2 * HALO, layer, 0)


def edges_kernel(
    z, line, place, tiles, start, same_chip, next_chip, speed_xi, speed_eta, matrix,
    low1, low2, dinv, up1, up2, inner, outer, ends, low, high, slope, keep, spread,
):
    first = place[1] == 0
    edge, wide = HALO * z.layer, 2 * HALO * z.layer
    low[0:edge, :] = jnp.where(place[0] == 0, 0.0, jnp.where(first, next_chip[...], same_chip[...]))
    low[edge : edge + wide, :] = tiles[edge : edge + wide, :]
    after = jnp.where(first, same_chip[...], next_chip[...])
    high[wide : wide + edge, :] = jnp.where(place[0] == line - 1, 0.0, after)
    high[0:wide, :] = tiles[z.rows - edge - wide : z.rows - edge, :]
    columns = flux_columns(z, matrix)
    for n in range(HALO):
        at, to = (n + HALO) * z.layer, n * z.layer
        residual_layer(z, n, low, at, start, speed_xi, speed_eta, columns, slope, outer, to)
        i = z.cl - HALO + n
        residual_layer(z, i, high, at, start, speed_xi, speed_eta, columns, slope, outer, edge + to)
    nothing = jnp.zeros((SUB, LANES), F32)
    for h in range(z.halves):
        states = [(nothing, nothing)] * SUB
        for i in range(z.cl):
            states = [lower_at(z, (inner, outer), low1, low2, dinv, keep, states[j], i, h, j) for j in range(SUB)]
        lowered = states
        states = [(nothing, nothing)] * SUB
        for i in reversed(range(z.cl)):
            states = [upper_at(z, keep, up1, up2, states[j], i, h, j) for j in range(SUB)]
        for j in range(SUB):
            for v, value in enumerate((*lowered[j], *states[j])):
                spread[pl.ds((h * SUB * 4 + v) * SUB + j, SUB, stride=4 * SUB), :] = value
        size = z.fields * 4 * SUB
        ends[h * size : (h + 1) * size, :] = spread[h * SUB * 4 * SUB : h * SUB * 4 * SUB + size, :]


def solve_kernel(z, chips, last, *refs):
    place, refs = refs[0], refs[1:]
    own, other, own_maps, other_maps, chip_ends, chip_maps = refs[:6]
    far, far_maps, refs = refs[6 : 4 + 2 * chips], refs[4 + 2 * chips : 2 + 4 * chips], refs[2 + 4 * chips :]
    rhs, refs = refs[:2], refs[2:]
    (tiles, low1, low2, dinv, up1, up2, e_low1, e_low2, e_dinv, e_up1, e_up2), refs = refs[:11], refs[11:]
    if last:
        out, states, planes, spread, keep, fresh = refs
    else:
        donor, weight, out, tiles_out, states, planes, spread, keep, fresh, picks, picks_b, where, *rest = refs
    core, chip = place[1], place[2]
    first = core == 0
    s_rows, m_rows = z.fields * 4 * SUB, MAPS * SUB

    def put(ref, at_chip, half, rows, source, begin):
        at = (at_chip * z.halves + half) * rows
        ref[pl.ds(pl.multiple_of(at, SUB), rows), :] = source[begin : begin + rows, :]

    for half in range(z.halves):
        put(states, chip, half, s_rows, chip_ends, half * s_rows)
        put(planes, chip, half, m_rows, chip_maps, half * m_rows)
    for s in range(1, chips):
        for t in range(2):
            put(states, chip ^ s, core ^ t, s_rows, far[2 * (s - 1) + t], 0)
            put(planes, chip ^ s, core ^ t, m_rows, far_maps[2 * (s - 1) + t], s_rows)

    zero = jnp.zeros((SUB, LANES), F32)
    for h in range(z.halves):

        def plane(at, p):
            row = ((at * z.halves + h) * MAPS + p) * SUB
            return planes[row : row + SUB, :]

        def end(at, f, v):
            row = ((at * z.halves + h) * z.fields * 4 + f * 4 + v) * SUB
            return states[row : row + SUB, :]

        entering = [[(zero, zero)] for _ in range(z.fields)]
        for d in range(chips - 1):
            for f in range(z.fields):
                a, b = entering[f][-1]
                entering[f].append(
                    (
                        end(d, f, 0) + plane(d, 0) * a + plane(d, 1) * b,
                        end(d, f, 1) + plane(d, 2) * a + plane(d, 3) * b,
                    )
                )
        mine = [[zero] * 4 for _ in range(z.fields)]
        returning = [(zero, zero)] * z.fields
        for d in reversed(range(chips)):
            for f in range(z.fields):
                a, b = entering[f][d]
                g, k = returning[f]
                mine[f] = [jnp.where(chip == d, new, old) for new, old in zip((a, b, g, k), mine[f])]
                returning[f] = (
                    (end(d, f, 2) + plane(d, 4) * a + plane(d, 5) * b) + (plane(d, 8) * g + plane(d, 9) * k),
                    (end(d, f, 3) + plane(d, 6) * a + plane(d, 7) * b) + (plane(d, 10) * g + plane(d, 11) * k),
                )

        def pick(left, one, two, row):
            return jnp.where(first == left, one[row : row + SUB, :], two[row : row + SUB, :])

        l = [pick(True, own_maps, other_maps, (h * MAPS + p) * SUB) for p in range(4)]
        r = [pick(False, own_maps, other_maps, (h * MAPS + p) * SUB) for p in range(MAPS)]
        for f in range(SUB):
            at = h * SUB * 4 + f * 4
            if f < z.fields:
                a, b, g, k = mine[f]
                rows = [((h * z.fields + f) * 4 + v) * SUB for v in range(4)]
                c = pick(True, own, other, rows[0]) + l[0] * a + l[1] * b
                d = pick(True, own, other, rows[1]) + l[2] * a + l[3] * b
                m = (pick(False, own, other, rows[2]) + r[4] * c + r[5] * d) + (r[8] * g + r[9] * k)
                n = (pick(False, own, other, rows[3]) + r[6] * c + r[7] * d) + (r[10] * g + r[11] * k)
                values = [jnp.where(first, a, c), jnp.where(first, b, d), jnp.where(first, m, g), jnp.where(first, n, k)]
            else:
                values = [zero] * 4
            for v in range(4):
                spread[(at + v) * SUB : (at + v + 1) * SUB, :] = values[v]

    def enter(v, h, j):
        return spread[pl.ds((h * SUB * 4 + v) * SUB + j, SUB, stride=4 * SUB), :]

    if not last:
        fresh[0 : HALO * z.layer, :] = jnp.zeros((HALO * z.layer, LANES), F32)
        fresh[z.rows - HALO * z.layer : z.rows, :] = jnp.zeros((HALO * z.layer, LANES), F32)
    for h in range(z.halves):
        state = [(enter(0, h, j), enter(1, h, j)) for j in range(SUB)]
        for i in range(z.cl):
            state = [lower_at(z, rhs, low1, low2, dinv, keep, state[j], i, h, j) for j in range(SUB)]
        state = [(enter(2, h, j), enter(3, h, j)) for j in range(SUB)]
        for i in reversed(range(z.cl)):
            state = [upper_at(z, keep, up1, up2, state[j], i, h, j) for j in range(SUB)]
            one, two = zero, zero
            lowered = []
            for j in range(SUB):
                new = line_of(e_dinv, i, h, j) * (
                    state[j][0] - line_of(e_low1, i, h, j) * one - line_of(e_low2, i, h, j) * two
                )
                one, two = new, one
                lowered.append(new)
            one, two = zero, zero
            for j in reversed(range(SUB)):
                new = lowered[j] - line_of(e_up1, i, h, j) * one - line_of(e_up2, i, h, j) * two
                one, two = new, one
                row = z.at(i + HALO, h, j)
                fresh[row : row + SUB, :] = tiles[row : row + SUB, :] + new
    if last:
        for f in range(z.fields):
            for i in range(z.cl):
                for h in range(z.halves):
                    out[f, i, :, h * LANES : (h + 1) * LANES] = fresh[
                        pl.ds(z.at(i + HALO, h, 0) + f, SUB, stride=SUB), :
                    ]
    else:
        tiles_out[...] = fresh[...]
        gather_all(z, donor, weight, fresh, out, (picks, picks_b), where, rest[:SLOTS], rest[SLOTS])


def to_other_core(array):
    return lax.ppermute(array, "line", [(i, i ^ 1) for i in range(lax.axis_size("line"))])


def from_other_chips(array):
    size = lax.axis_size("line")
    result = []
    for s in range(1, size // 2):
        there = lax.ppermute(array, "line", [(i, i ^ (2 * s)) for i in range(size)])
        result += [there, to_other_core(there)]
    return result


def local(
    conserved, flux_matrix, speed_xi, speed_eta, x_low1, x_low2, x_dinv, x_up1, x_up2,
    e_low1, e_low2, e_dinv, e_up1, e_up2, donor_index, donor_weight, receive_index,
):
    z = Sizes(*conserved.shape)
    count = lax.axis_size("line")
    devices = count * lax.axis_size("batch")
    corners, fringe = donor_index.shape
    assert fringe == devices * (LANES // 2) and count % 2 == 0 and count & (count - 1) == 0
    blocks = fringe // LANES
    me = lax.axis_index("line").astype(I32)
    place = jnp.stack([me, me & 1, me >> 1])
    matrix = jnp.pad(flux_matrix, ((0, SUB - z.fields), (0, LANES - z.fields)))
    receive = receive_index.reshape(blocks, LANES)
    x_coefs = (x_low1, x_low2, x_dinv, x_up1, x_up2)
    e_coefs = (e_low1, e_low2, e_dinv, e_up1, e_up2)
    params = pltpu.CompilerParams(vmem_limit_bytes=32 * 1024 * 1024)
    picked = f32(blocks * SUB, LANES)
    tile_shape = f32(z.rows, LANES)
    tile_mem = pltpu.VMEM((z.rows, LANES), F32)
    inner_mem = pltpu.VMEM((z.cl * z.layer, LANES), F32)
    spread_mem = pltpu.VMEM((SUB * 4 * z.columns, LANES), F32)
    s_rows, m_rows = z.fields * 4 * SUB, MAPS * SUB
    chips = count // 2
    assert z.halves == 2

    maps = pl.pallas_call(
        functools.partial(segment_kernel, z),
        out_shape=f32(z.halves * m_rows, LANES),
        in_specs=[VM] * 5,
        out_specs=VM,
        compiler_params=params,
        name="segments",
    )(*x_coefs)
    other_maps = to_other_core(maps)

    values, tiles = pl.pallas_call(
        functools.partial(first_kernel, z),
        out_shape=[picked, tile_shape],
        in_specs=[VM] * 3,
        out_specs=[VM] * 2,
        scratch_shapes=[tile_mem, *gather_scratch(corners, fringe)],
        compiler_params=params,
        name="donors",
    )(donor_index, donor_weight, conserved)
    start = tiles

    for sweep in range(SUBITERS):
        last = sweep == SUBITERS - 1
        inbound = lax.all_to_all(values.reshape(devices, 4, LANES), ("line", "batch"), 0, 0, tiled=True)
        inbound = inbound.reshape(blocks * SUB, LANES)
        tiles, same_chip, next_chip = pl.pallas_call(
            functools.partial(place_kernel, z),
            out_shape=[tile_shape, f32(HALO * z.layer, LANES), f32(HALO * z.layer, LANES)],
            in_specs=[SM] + [VM] * 3,
            out_specs=[VM] * 3,
            scratch_shapes=[
                pltpu.VMEM((blocks * SUB, LANES), I32),
                pltpu.VMEM((SLOTS * LANES, LANES), F32),
                *[pltpu.SMEM((SUB, LANES), I32) for _ in range(SLOTS)],
                pltpu.SemaphoreType.DMA((SLOTS,)),
            ],
            compiler_params=params,
            name="receivers",
        )(place, receive, inbound, tiles)
        same_chip = lax.ppermute(same_chip, "line", [(i, i ^ 1) for i in range(count)])
        facing = [(i, (i + 1) % count) for i in range(1, count, 2)]
        next_chip = lax.ppermute(next_chip, "line", facing + [(b, a) for a, b in facing])
        layers = z.cl - 2 * HALO
        inner = pl.pallas_call(
            functools.partial(interior_kernel, z),
            out_shape=f32(layers * z.layer, LANES),
            in_specs=[VM] * 5,
            out_specs=VM,
            scratch_shapes=[pltpu.VMEM((z.layer, LANES), F32)],
            compiler_params=params,
            cost_estimate=pl.CostEstimate(
                flops=layers * z.layer * LANES * 40, bytes_accessed=layers * z.layer * LANES * 16, transcendentals=0
            ),
            name="interior",
        )(tiles, start, speed_xi, speed_eta, matrix)
        outer, ends = pl.pallas_call(
            functools.partial(edges_kernel, z, count),
            out_shape=[f32(2 * HALO * z.layer, LANES), f32(z.halves * s_rows, LANES)],
            in_specs=[SM] + [VM] * 13,
            out_specs=[VM] * 2,
            scratch_shapes=[
                pltpu.VMEM((3 * HALO * z.layer, LANES), F32),
                pltpu.VMEM((3 * HALO * z.layer, LANES), F32),
                pltpu.VMEM((z.layer, LANES), F32),
                inner_mem,
                spread_mem,
            ],
            compiler_params=params,
            name="edges",
        )(place, tiles, start, same_chip, next_chip, speed_xi, speed_eta, matrix, *x_coefs, inner)
        other_ends = to_other_core(ends)
        with_maps = sweep == 0
        shapes = [f32(z.halves * s_rows, LANES)]
        if with_maps:
            shapes.append(f32(z.halves * m_rows, LANES))
        shapes.append(f32(s_rows + m_rows * with_maps, LANES))
        composed = pl.pallas_call(
            functools.partial(compose_kernel, z, with_maps),
            out_shape=shapes,
            in_specs=[SM] + [VM] * 4,
            out_specs=[VM] * len(shapes),
            compiler_params=params,
            name="compose",
        )(place, ends, other_ends, maps, other_maps)
        chip_ends, half = composed[0], composed[-1]
        far = from_other_chips(half)
        if with_maps:
            chip_maps, far_maps = composed[1], far
        scratch = [
            pltpu.VMEM((chips * z.halves * s_rows, LANES), F32),
            pltpu.VMEM((chips * z.halves * m_rows, LANES), F32),
            spread_mem,
            inner_mem,
            tile_mem,
        ]
        operands = (place, ends, other_ends, maps, other_maps, chip_ends, chip_maps, *far, *far_maps)
        operands = (*operands, inner, outer, tiles, *x_coefs, *e_coefs)
        if last:
            return pl.pallas_call(
                functools.partial(solve_kernel, z, chips, True),
                out_shape=f32(*conserved.shape),
                in_specs=[SM] + [VM] * (len(operands) - 1),
                out_specs=VM,
                scratch_shapes=scratch,
                compiler_params=params,
                name="solve_last",
            )(*operands)
        operands = (*operands, donor_index, donor_weight)
        values, tiles = pl.pallas_call(
            functools.partial(solve_kernel, z, chips, False),
            out_shape=[picked, tile_shape],
            in_specs=[SM] + [VM] * (len(operands) - 1),
            out_specs=[VM] * 2,
            scratch_shapes=[*scratch, *gather_scratch(corners, fringe)],
            compiler_params=params,
            name="solve_donors",
        )(*operands)


def solution(mesh):
    field = P(None, "line", None, "batch")
    coef = P("line", None, "batch")
    fringe = ("line", "batch")
    in_specs = (field, P(), *[coef] * 12, P(None, fringe), P(None, fringe), P(fringe))
    return jax.shard_map(local, mesh=mesh, in_specs=in_specs, out_specs=field, check_vma=False)
```
